32 devices in a mesh: dp: 4 (over z), expert: 8 (over y, x, core).
Axes of the slice: x: 2, y: 2, z: 4, core: 2. Of those that a mesh axis runs over, the one named last changes fastest.
Arguments:
- tokens: bfloat16 [1024, 3584], P('expert', 'dp'), may hold values from -6 to 6
- cotangent: bfloat16 [1024, 3584], P('expert', 'dp'), may hold values from -6 to 6
- routes: int32 [1024, 3], P('expert'), may hold values from 0 to 5, all different within a row; in each aligned block of 128 rows (0 to 127, 128 to 255, ...) at most 72 rows name the same one
- route_weight: float32 [1024, 3], P('expert'), may hold values from 0.1 to 0.6
- gate_weight: bfloat16 [8, 3584, 1024], P('expert', None, 'dp'), may hold values from -6 to 6
- up_weight: bfloat16 [8, 3584, 1024], P('expert', None, 'dp'), may hold values from -6 to 6
- down_weight: bfloat16 [8, 1024, 3584], P('expert', None, 'dp'), may hold values from -6 to 6
- first_moment: bfloat16 [8, 3584, 1024], P('expert', None, 'dp'), may hold values from -0.59765625 to 0.59765625
- second_moment: bfloat16 [8, 3584, 1024], P('expert', None, 'dp'), may hold values from 0.0009994507 to 0.029907227
- placement: int32 [8], replicated, may hold values from 0 to 5, as said below
- migration_plan: int32 [8], replicated, may hold values from 0 to 7, as said below
Outputs:
- layer_output: bfloat16 [1024, 3584], P('expert', 'dp')
- new_gate: bfloat16 [8, 3584, 1024], P('expert', None, 'dp')
- new_first: bfloat16 [8, 3584, 1024], P('expert', None, 'dp')
- new_second: bfloat16 [8, 3584, 1024], P('expert', None, 'dp')
The draws below stay inside these ranges and needn't reach their ends.
Inputs may be any that keep to these rules, and one draw needn't show every extreme that they name: `routes`: each row names 3 different experts; among the rows of one index of the expert axis no expert is named more than 72 times. `placement`: every expert from 0 to 5 is held by one slot or more. `migration_plan`: every expert keeps one slot or more in the new placement.
All inputs are finite; a program needn't handle non-finite values.
Results may differ from the reference program's by a relative error of at most 0.033.
Values may be sent and summed in bfloat16 or wider, within the bound.
A program may use at most 128 MiB of HBM per device.

```python
import math
import jax
import jax.numpy as jnp
import numpy as np
from jax import lax

D = 3584
FF = 1024
TOK_DEV = 128
EXPERTS = 6
TOP = 3
CAP = 72
TOKENS = 1024
N_DP = 4
N_EXPERT = 8


def placement_tables(key):
    key_order, key_extra = jax.random.split(jax.random.fold_in(key, 11))
    order = jax.random.permutation(key_order, N_EXPERT).astype(jnp.int32)
    extra = jax.random.randint(key_extra, (N_EXPERT,), 0, EXPERTS).astype(jnp.int32)
    ranks = jnp.arange(N_EXPERT, dtype=jnp.int32)
    expert_of_rank = jnp.where(ranks < EXPERTS, ranks, extra)
    placement = jnp.zeros((N_EXPERT,), jnp.int32).at[order].set(expert_of_rank)
    rank_of_slot = jnp.argsort(order, stable=True).astype(jnp.int32)
    return (placement, order, rank_of_slot)


def draw_placement(key, part):
    return placement_tables(key)[0]


def draw_migration_plan(key, part):
    placement, order, rank_of_slot = placement_tables(key)
    key_base, key_coin, key_primary = jax.random.split(jax.random.fold_in(key, 23), 3)
    base = jax.random.permutation(key_base, N_EXPERT).astype(jnp.int32)
    is_extra = rank_of_slot[base] >= EXPERTS
    coin = jax.random.randint(key_coin, (N_EXPERT,), 0, 2) == 1
    primary = order[jax.random.randint(key_primary, (N_EXPERT,), 0, EXPERTS)]
    return jnp.where(is_extra & coin, primary, base).astype(jnp.int32)


def level_of(key, dims, cuts, low, largest):
    def one(dim, parts):
        draws = jax.random.uniform(jax.random.fold_in(jax.random.fold_in(key, 6), dim), (parts,), jnp.float32, low / len(cuts), largest / len(cuts))
        return jnp.repeat(jnp.exp(draws), dims[dim] // parts).reshape((-1,) + (1,) * (len(dims) - dim - 1))

    gain = one(*cuts[0])
    for cut in cuts[1:]:
        gain = gain * one(*cut)
    return gain


def deal_out(stream_key, own, number, rows, amount, top, most, skew):
    sequence = jax.random.permutation(stream_key, amount)
    heavy_load, common = portions_of(amount, rows * top, most, skew, True), portions_of(amount, rows * top, most, skew, False)
    places = jnp.arange(amount)

    def named(lengths, rotation):
        used = int((lengths > 0).sum())
        fixed = max(1, used // 4)
        shifted = fixed + (places - fixed + rotation * (used - fixed)) % max(1, amount - fixed)
        return jnp.zeros((amount,), jnp.int32).at[sequence[jnp.where(places < fixed, places, shifted)]].set(jnp.asarray(lengths, jnp.int32))

    lengths = jnp.where(number % 4 == 0, named(heavy_load, number // 4), named(common, number - number // 4 - 1))
    mixed = jax.random.permutation(jax.random.fold_in(own, 3), amount)
    source_of, taker = mixed[0:amount // 2 * 2:2], mixed[1:amount // 2 * 2:2]
    margin = jnp.minimum(lengths[source_of] - 1, most - lengths[taker]) // 2
    margin = jnp.where((source_of == sequence[0]) | (taker == sequence[0]) | (lengths[taker] == 0), 0, jnp.maximum(margin, 0))
    shifted = jax.random.randint(jax.random.fold_in(own, 4), (amount // 2,), 0, 1 << 20) % (margin + 1)
    lengths = lengths.at[source_of].add(-shifted).at[taker].add(shifted)
    labels = jnp.searchsorted(jnp.cumsum(lengths), jnp.arange(rows * top), side="right").astype(jnp.int32)
    grid = labels.reshape(top, rows).T
    grid = grid[jax.random.permutation(jax.random.fold_in(own, 1), rows)]
    rotation = jax.random.randint(jax.random.fold_in(own, 2), (rows, 1), 0, top)
    return jnp.take_along_axis(grid, (jnp.arange(top)[None, :] + rotation) % top, axis=1)


def portions_of(amount, total, bound, skew, full):
    portions = [(1 << 20) // math.isqrt(rank ** skew) + 1 for rank in range(1, amount + 1)]
    largest = bound if full else min(bound, max(-(-total // amount), total * portions[0] // sum(portions)))
    least = 1 if total - largest >= amount - 1 else 0
    counts, spare = [largest] + [least] * (amount - 1), total - largest - least * (amount - 1)
    while spare > 0:
        movable = [i for i in range(1, amount) if counts[i] < largest] or [i for i in range(1, amount) if counts[i] < bound]
        mass, budget = sum([portions[i] for i in movable]), spare
        for i in movable:
            more = min(bound - counts[i], max(1, budget * portions[i] // mass), spare)
            counts[i] = counts[i] + more
            spare = spare - more
    return np.array(counts)


def scatter_about(rng, shape, spread, most, cuts=(), held_as=jnp.bfloat16):
    factor_of = level_of(rng, shape, cuts, -0.22, 0.18) if cuts else 1.0
    array = jax.random.normal(rng, shape, jnp.float32) * spread * factor_of
    return jnp.minimum(jnp.maximum(array, -most), most).astype(held_as)


def setup_inputs(seed: int = 0) -> dict:
    seeds = jax.random.split(jax.random.key(seed), 12)
    tokens = scatter_about(seeds[0], (TOKENS, D), 1.0, 6.0, ((0, 8), (1, 4)))
    cotangent = scatter_about(seeds[1], (TOKENS, D), 1.0, 6.0, ((0, 8), (1, 4)))
    routes_keys = jax.random.split(jax.random.fold_in(seeds[2], 1), TOKENS // TOK_DEV)
    routes_turns = jax.random.permutation(jax.random.fold_in(seeds[2], 3), TOKENS // TOK_DEV)
    routes = jax.vmap(lambda own, number: deal_out(jax.random.fold_in(seeds[2], 2), own, number, TOK_DEV, EXPERTS, TOP, CAP, 2))(routes_keys, routes_turns).reshape((TOKENS, TOP))
    route_weight = jnp.clip(0.1 + 0.5 * jax.random.uniform(seeds[3], (TOKENS, TOP), jnp.float32) ** level_of(seeds[3], (TOKENS, TOP), ((0, 8),), -0.2, 0.2), 0.1, 0.6)
    gate_weight = scatter_about(seeds[4], (N_EXPERT, D, FF), 1.0, 6.0, ((0, 8), (2, 4)))
    up_weight = scatter_about(seeds[5], (N_EXPERT, D, FF), 1.0, 6.0, ((0, 8), (2, 4)))
    down_weight = scatter_about(seeds[6], (N_EXPERT, FF, D), 1.0, 6.0, ((0, 8), (2, 4)))
    first_moment = scatter_about(seeds[7], (N_EXPERT, D, FF), 0.1, 0.59765625, ((0, 8), (2, 4)))
    second_moment = jnp.clip(jnp.exp(math.log(0.029907227) - 3.3986496 * jax.random.uniform(seeds[8], (N_EXPERT, D, FF), jnp.float32) ** level_of(seeds[8], (N_EXPERT, D, FF), ((0, 8), (2, 4)), -0.2, 0.2)), 0.0009994507, 0.029907227).astype(jnp.bfloat16)
    placement = draw_placement(jax.random.fold_in(seeds[11], 71), 0)
    migration_plan = draw_migration_plan(jax.random.fold_in(seeds[11], 71), 0)
    return dict(tokens=tokens, cotangent=cotangent, routes=routes, route_weight=route_weight, gate_weight=gate_weight, up_weight=up_weight, down_weight=down_weight, first_moment=first_moment, second_moment=second_moment, placement=placement, migration_plan=migration_plan)


beta_first = 0.9
beta_second = 0.95
learn_rate = 0.02
weight_decay = 0.1
epsilon = 1e-08

def choose_slots(routes, placement, source):
    slot_iota = jnp.arange(placement.shape[0], dtype=jnp.int32)
    hosting = routes[..., None] == placement
    copies = lax.optimization_barrier(jnp.sum(hosting, -1)).astype(jnp.int32)
    earlier = (placement[:, None] == placement[None, :]) & (slot_iota[:, None] < slot_iota[None, :])
    replica_rank = lax.optimization_barrier(jnp.sum(earlier, 0)).astype(jnp.int32)
    replica = source[:, None] % copies
    matched = hosting & (replica_rank == replica[..., None])
    return lax.optimization_barrier(jnp.sum(jnp.where(matched, slot_iota, 0), -1)).astype(jnp.int32)

def place_rows(slot_ids, slot_count):
    tok_rows, per_token = slot_ids.shape
    flattened = slot_ids.reshape(-1)
    onehot = (flattened[:, None] == jnp.arange(slot_count, dtype=jnp.int32)).astype(jnp.int32)
    running = jnp.cumsum(onehot, 0)
    return (lax.optimization_barrier(jnp.sum(running * onehot, 1)) - 1).astype(jnp.int32).reshape(tok_rows, per_token)

def adam_update(gradient, weight, first_old, second):
    moment_one = beta_first * first_old.astype(jnp.float32) + (1.0 - beta_first) * gradient
    moment_two = beta_second * second.astype(jnp.float32) + (1.0 - beta_second) * gradient * gradient
    updated = weight.astype(jnp.float32) * (1.0 - learn_rate * weight_decay) - learn_rate * moment_one / (jnp.sqrt(moment_two) + epsilon)
    return (updated, moment_one, moment_two)

def reference(tokens, cotangent, routes, route_weight, gate_weight, up_weight, down_weight, first_moment, second_moment, placement, migration_plan):
    scale_in = 1.0 / math.sqrt(D)
    scale_mid = 1.0 / math.sqrt(FF)
    quarter = D // N_DP
    source = (jnp.arange(TOKENS, dtype=jnp.int32) // TOK_DEV).astype(jnp.int32)
    slot_ids = choose_slots(routes, placement, source)

    def block_rows(block):
        return place_rows(block, N_EXPERT)
    position = jax.vmap(block_rows)(slot_ids.reshape(N_EXPERT, TOK_DEV, TOP)).reshape(TOKENS, TOP)
    buffer_row = (source[:, None] * CAP + position).astype(jnp.int32)
    token_buffer = jnp.zeros((N_EXPERT, N_EXPERT * CAP, D), jnp.bfloat16)
    grad_buffer = jnp.zeros((N_EXPERT, N_EXPERT * CAP, D), jnp.bfloat16)
    for route_index in range(TOP):
        token_buffer = token_buffer.at[slot_ids[:, route_index], buffer_row[:, route_index]].set(tokens)
        scaled = (route_weight[:, route_index:route_index + 1] * cotangent.astype(jnp.float32)).astype(jnp.bfloat16)
        grad_buffer = grad_buffer.at[slot_ids[:, route_index], buffer_row[:, route_index]].set(scaled)

    def expert_step(operands):
        inputs, upstream, w_gate, w_up, w_down = operands
        gate_values = jnp.dot(inputs, w_gate, preferred_element_type=jnp.float32) * scale_in
        up_values = jnp.dot(inputs, w_up, preferred_element_type=jnp.float32) * scale_in
        hidden = (jax.nn.silu(gate_values) * up_values).astype(jnp.bfloat16)
        outputs = (jnp.dot(hidden, w_down, preferred_element_type=jnp.float32) * scale_mid).astype(jnp.bfloat16)
        hidden_grad = jnp.zeros(gate_values.shape, jnp.float32)
        for quarter_index in range(N_DP):
            lower = quarter_index * quarter
            partial_grad = jnp.dot(upstream[:, lower:lower + quarter], w_down[:, lower:lower + quarter].T, preferred_element_type=jnp.float32)
            hidden_grad = hidden_grad + partial_grad.astype(jnp.bfloat16).astype(jnp.float32)
        hidden_grad = hidden_grad * scale_mid
        sigmoid_gate = jax.nn.sigmoid(gate_values)
        gate_grad = (hidden_grad * up_values * sigmoid_gate * (1.0 + gate_values * (1.0 - sigmoid_gate))).astype(jnp.bfloat16)
        weight_grad = jnp.dot(inputs.T, gate_grad, preferred_element_type=jnp.float32) * scale_in
        return (outputs, weight_grad)
    expert_out, slot_grad = lax.map(expert_step, (token_buffer, grad_buffer, gate_weight, up_weight, down_weight))
    combined = jnp.zeros((TOKENS, D), jnp.float32)
    for route_index in range(TOP):
        rows_back = expert_out[slot_ids[:, route_index], buffer_row[:, route_index]].astype(jnp.float32)
        combined = combined + route_weight[:, route_index:route_index + 1] * rows_back
    layer_output = combined.astype(jnp.bfloat16)
    same_expert = (placement[:, None] == placement[None, :]).astype(jnp.float32)
    expert_grad = jnp.dot(same_expert, slot_grad.reshape(N_EXPERT, -1), precision=lax.Precision.HIGHEST).reshape(slot_grad.shape)
    updated, first, second = adam_update(expert_grad, gate_weight, first_moment, second_moment)
    new_gate = updated[migration_plan].astype(jnp.bfloat16)
    new_first = first[migration_plan].astype(jnp.bfloat16)
    new_second = second[migration_plan].astype(jnp.bfloat16)
    return (layer_output, new_gate, new_first, new_second)
```

```python
import math

import jax
import jax.numpy as jnp
from jax import lax
from jax.experimental import pallas as pl
from jax.experimental.pallas import tpu as pltpu
from jax.sharding import PartitionSpec as P

D = 3584
FF = 1024


beta_first = 0.9
beta_second = 0.95
learn_rate = 0.02
weight_decay = 0.1
epsilon = 1e-08


def choose_slots(routes, placement, source):
    slot_iota = jnp.arange(placement.shape[0], dtype=jnp.int32)
    hosting = routes[..., None] == placement
    copies = jnp.sum(hosting, -1)
    earlier = (placement[:, None] == placement[None, :]) & (slot_iota[:, None] < slot_iota[None, :])
    replica_rank = jnp.sum(earlier, 0)
    replica = source[:, None] % copies
    matched = hosting & (replica_rank == replica[..., None])
    return jnp.sum(jnp.where(matched, slot_iota, 0), -1)


def place_rows(slot_ids, slot_count):
    tok_rows, per_token = slot_ids.shape
    flattened = slot_ids.reshape(-1)
    onehot = (flattened[:, None] == jnp.arange(slot_count, dtype=jnp.int32)).astype(jnp.int32)
    count = flattened.shape[0]
    order = jnp.arange(count, dtype=jnp.int32)
    upto = (order[:, None] >= order[None, :]).astype(jnp.bfloat16)
    running = jnp.dot(
        upto, onehot.astype(jnp.bfloat16), preferred_element_type=jnp.float32
    ).astype(jnp.int32)
    return (jnp.sum(running * onehot, 1) - 1).reshape(tok_rows, per_token)


def adam_update(gradient, weight, first_old, second):
    moment_one = beta_first * first_old.astype(jnp.float32) + (1.0 - beta_first) * gradient
    moment_two = (
        beta_second * second.astype(jnp.float32) + (1.0 - beta_second) * gradient * gradient
    )
    updated = weight.astype(jnp.float32) * (
        1.0 - learn_rate * weight_decay
    ) - learn_rate * moment_one / (jnp.sqrt(moment_two) + epsilon)
    return (
        updated.astype(jnp.bfloat16),
        moment_one.astype(jnp.bfloat16),
        moment_two.astype(jnp.bfloat16),
    )


def update_kernel(
    placement_ref, plan_ref, weight_ref, first_ref, second_ref, grad_ref, out_w, out_1, out_2
):
    held = placement_ref[plan_ref[pl.program_id(0)]]
    slots, rows, _ = grad_ref.shape
    chunk = math.gcd(rows, 112)

    @pl.loop(0, rows // chunk)
    def _(step):
        part = pl.ds(pl.multiple_of(step * chunk, chunk), chunk)
        gradient = jnp.zeros((chunk, grad_ref.shape[2]), jnp.float32)
        for slot in range(slots):
            share = jnp.where(placement_ref[slot] == held, 1.0, 0.0).astype(jnp.float32)
            gradient = gradient + share * grad_ref[slot, part].astype(jnp.float32)
        out_w[0, part], out_1[0, part], out_2[0, part] = adam_update(
            gradient, weight_ref[0, part], first_ref[0, part], second_ref[0, part]
        )


def update_slots(placement, plan, weight, first, second, grads):
    slots, rows, columns = weight.shape
    taken = pl.BlockSpec((1, rows, columns), lambda s, held, plan: (plan[s], 0, 0))
    every = pl.BlockSpec((slots, rows, columns), lambda s, held, plan: (0, 0, 0))
    made = pl.BlockSpec((1, rows, columns), lambda s, held, plan: (s, 0, 0))
    return pl.pallas_call(
        update_kernel,
        out_shape=[jax.ShapeDtypeStruct(weight.shape, jnp.bfloat16)] * 3,
        grid_spec=pltpu.PrefetchScalarGridSpec(
            num_scalar_prefetch=2,
            grid=(slots,),
            in_specs=[taken, taken, taken, every],
            out_specs=[made, made, made],
        ),
        compiler_params=pltpu.CompilerParams(vmem_limit_bytes=32 * 2**20),
        cost_estimate=pl.CostEstimate(
            flops=30 * weight.size, bytes_accessed=14 * weight.size, transcendentals=weight.size
        ),
    )(placement, plan, weight, first, second, grads)


def per_device(
    tokens,
    cotangent,
    routes,
    route_weight,
    gate_weight,
    up_weight,
    down_weight,
    first_moment,
    second_moment,
    placement,
    migration_plan,
):
    slot_count = lax.axis_size("expert")
    device_index = lax.axis_index("expert")
    tok_rows, quarter = tokens.shape
    per_token = routes.shape[1]
    capacity = min(tok_rows, 3 * tok_rows * per_token // (2 * slot_count))
    buffer_size = slot_count * capacity
    scale_in = 1.0 / math.sqrt(D)
    scale_mid = 1.0 / math.sqrt(FF)
    source = jnp.full((tok_rows,), device_index, jnp.int32)
    slot_ids = choose_slots(routes, placement, source)
    position = place_rows(slot_ids, slot_count)
    target = slot_ids * capacity + position
    buffer_slots = jnp.arange(buffer_size, dtype=jnp.int32)
    landing = target[None, :, :] == buffer_slots[:, None, None]
    selection = jnp.any(landing, -1).astype(jnp.bfloat16)
    row_weight = jnp.sum(jnp.where(landing, route_weight[None], jnp.float32(0.0)), (1, 2))
    sent_rows = jnp.dot(selection, tokens, preferred_element_type=jnp.float32).astype(jnp.bfloat16)
    picked_grads = jnp.dot(selection, cotangent, preferred_element_type=jnp.float32)
    sent_grads = (row_weight[:, None] * picked_grads).astype(jnp.bfloat16)
    sent_rows = sent_rows.reshape(slot_count, capacity, quarter)
    sent_grads = sent_grads.reshape(slot_count, capacity, quarter)
    got_rows, got_grads = (
        lax.all_to_all(sent_rows, "expert", split_axis=0, concat_axis=0, tiled=True),
        lax.all_to_all(sent_grads, "expert", split_axis=0, concat_axis=0, tiled=True),
    )
    inputs = lax.all_gather(got_rows.reshape(buffer_size, quarter), "dp", axis=1, tiled=True)
    gate_values = jnp.dot(inputs, gate_weight[0], preferred_element_type=jnp.float32) * scale_in
    up_values = jnp.dot(inputs, up_weight[0], preferred_element_type=jnp.float32) * scale_in
    hidden = (jax.nn.silu(gate_values) * up_values).astype(jnp.bfloat16)
    every_hidden = lax.all_gather(hidden, "dp", axis=1, tiled=True)
    w_down = down_weight[0]
    outputs = (
        jnp.dot(every_hidden, w_down, preferred_element_type=jnp.float32) * scale_mid
    ).astype(jnp.bfloat16)
    returned = lax.all_to_all(
        outputs.reshape(slot_count, capacity, quarter),
        "expert",
        split_axis=0,
        concat_axis=0,
        tiled=True,
    )
    returned_rows = returned.reshape(buffer_size, quarter)
    combined = jnp.zeros((tok_rows, quarter), jnp.float32)
    for route_index in range(per_token):
        rows_back = jnp.take(returned_rows, target[:, route_index], axis=0).astype(jnp.float32)
        combined = combined + route_weight[:, route_index : route_index + 1] * rows_back
    layer_output = combined.astype(jnp.bfloat16)
    partial_grad = lax.dot_general(
        got_grads.reshape(buffer_size, quarter),
        w_down,
        (((1,), (1,)), ((), ())),
        preferred_element_type=jnp.float32,
    )
    hidden_grad = (
        lax.psum_scatter(
            partial_grad.astype(jnp.bfloat16), "dp", scatter_dimension=1, tiled=True
        ).astype(jnp.float32)
        * scale_mid
    )
    sigmoid_gate = jax.nn.sigmoid(gate_values)
    gate_grad = (
        hidden_grad * up_values * sigmoid_gate * (1.0 + gate_values * (1.0 - sigmoid_gate))
    ).astype(jnp.bfloat16)
    weight_grad = (
        lax.dot_general(
            inputs, gate_grad, (((0,), (0,)), ((), ())), preferred_element_type=jnp.float32
        )
        * scale_in
    )
    def exchange(array):
        split = array.reshape(slot_count, array.shape[-2] // slot_count, array.shape[-1])
        return lax.all_to_all(split, "expert", split_axis=0, concat_axis=0, tiled=True)

    state_parts = [exchange(array[0]) for array in (gate_weight, first_moment, second_moment)]
    grad_parts = exchange(weight_grad.astype(jnp.bfloat16))
    updated = update_slots(placement, migration_plan, *state_parts, grad_parts)
    result = [
        lax.all_to_all(array, "expert", split_axis=0, concat_axis=0, tiled=True).reshape(
            first_moment.shape
        )
        for array in updated
    ]
    return (layer_output, result[0], result[1], result[2])


def solution(mesh):
    placed = (
        P("expert", "dp"),
        P("expert", "dp"),
        P("expert", None),
        P("expert", None),
        P("expert", None, "dp"),
        P("expert", None, "dp"),
        P("expert", None, "dp"),
        P("expert", None, "dp"),
        P("expert", None, "dp"),
        P(),
        P(),
    )
    return jax.shard_map(
        per_device,
        mesh=mesh,
        in_specs=placed,
        out_specs=(
            P("expert", "dp"),
            P("expert", None, "dp"),
            P("expert", None, "dp"),
            P("expert", None, "dp"),
        ),
        check_vma=False,
    )
```

```python
import math

import jax
import jax.numpy as jnp
from jax import lax
from jax.experimental import pallas as pl
from jax.experimental.pallas import tpu as pltpu
from jax.sharding import PartitionSpec as P

D = 3584
FF = 1024
MESH = pl.DeviceIdType.MESH


beta_first = 0.9
beta_second = 0.95
learn_rate = 0.02
weight_decay = 0.1
epsilon = 1e-08


def choose_slots(routes, placement, source):
    slot_iota = jnp.arange(placement.shape[0], dtype=jnp.int32)
    hosting = routes[..., None] == placement
    copies = jnp.sum(hosting, -1)
    earlier = (placement[:, None] == placement[None, :]) & (slot_iota[:, None] < slot_iota[None, :])
    replica_rank = jnp.sum(earlier, 0)
    replica = source[:, None] % copies
    matched = hosting & (replica_rank == replica[..., None])
    return jnp.sum(jnp.where(matched, slot_iota, 0), -1)


def place_rows(slot_ids, slot_count):
    tok_rows, per_token = slot_ids.shape
    flattened = slot_ids.reshape(-1)
    onehot = (flattened[:, None] == jnp.arange(slot_count, dtype=jnp.int32)).astype(jnp.int32)
    count = flattened.shape[0]
    order = jnp.arange(count, dtype=jnp.int32)
    upto = (order[:, None] >= order[None, :]).astype(jnp.bfloat16)
    running = jnp.dot(
        upto, onehot.astype(jnp.bfloat16), preferred_element_type=jnp.float32
    ).astype(jnp.int32)
    return (jnp.sum(running * onehot, 1) - 1).reshape(tok_rows, per_token)


def adam_update(gradient, weight, first_old, second):
    moment_one = beta_first * first_old.astype(jnp.float32) + (1.0 - beta_first) * gradient
    moment_two = (
        beta_second * second.astype(jnp.float32) + (1.0 - beta_second) * gradient * gradient
    )
    updated = weight.astype(jnp.float32) * (
        1.0 - learn_rate * weight_decay
    ) - learn_rate * moment_one / (jnp.sqrt(moment_two) + epsilon)
    return (
        updated.astype(jnp.bfloat16),
        moment_one.astype(jnp.bfloat16),
        moment_two.astype(jnp.bfloat16),
    )


def tail_kernel(
    placement_ref, plan_ref, weight_ref, first_ref, second_ref, grad_ref,
    out_w, out_1, out_2,
    state, got, staged, load_sem, grad_send, grad_recv, out_send, out_recv,
):
    slots, rows, columns = got.shape
    me = lax.axis_index("expert")
    outs = (out_w, out_1, out_2)
    chunk = math.gcd(rows, 112)

    loads = [
        pltpu.make_async_copy(ref, state.at[i], load_sem.at[i])
        for i, ref in enumerate((weight_ref, first_ref, second_ref))
    ]
    for load in loads:
        load.start()
    own = pltpu.make_async_copy(grad_ref.at[me], got.at[me], load_sem.at[3])
    own.start()

    barrier = pltpu.get_barrier_semaphore()

    @pl.loop(1, slots)
    def _(k):
        pl.semaphore_signal(
            barrier, inc=1, device_id={"expert": lax.rem(me + k, slots)}, device_id_type=MESH
        )

    pl.semaphore_wait(barrier, slots - 1)

    def grad_copy(k):
        peer = lax.rem(me + k, slots)
        return pltpu.make_async_remote_copy(
            src_ref=grad_ref.at[peer],
            dst_ref=got.at[me],
            send_sem=grad_send.at[k],
            recv_sem=grad_recv.at[k],
            device_id={"expert": peer},
            device_id_type=MESH,
        )

    def out_copy(k, i):
        return pltpu.make_async_remote_copy(
            src_ref=staged.at[i, k],
            dst_ref=outs[i].at[me],
            send_sem=out_send.at[i, k],
            recv_sem=out_recv.at[i, k],
            device_id={"expert": lax.rem(me + k, slots)},
            device_id_type=MESH,
        )

    @pl.loop(1, slots)
    def _(k):
        grad_copy(k).start()

    for load in loads:
        load.wait()
    own.wait()

    @pl.loop(1, slots)
    def _(k):
        grad_copy(k).wait()

    def work_out(k):
        old = plan_ref[lax.rem(me + k, slots)]
        held = placement_ref[old]
        shares = [
            jnp.where(placement_ref[slot] == held, 1.0, 0.0).astype(jnp.float32)
            for slot in range(slots)
        ]

        @pl.loop(0, rows // chunk)
        def _(step):
            part = pl.ds(pl.multiple_of(step * chunk, chunk), chunk)
            gradient = jnp.zeros((chunk, columns), jnp.float32)
            for slot in range(slots):
                gradient = gradient + shares[slot] * got[slot, part].astype(jnp.float32)
            staged[0, k, part], staged[1, k, part], staged[2, k, part] = adam_update(
                gradient, state[0, old, part], state[1, old, part], state[2, old, part]
            )

    @pl.loop(1, slots)
    def _(k):
        work_out(k)
        for i in range(3):
            out_copy(k, i).start()

    work_out(0)
    kept = [
        pltpu.make_async_copy(staged.at[i, 0], outs[i].at[me], load_sem.at[i]) for i in range(3)
    ]
    for copy in kept:
        copy.start()
    for copy in kept:
        copy.wait()

    @pl.loop(1, slots)
    def _(k):
        for i in range(3):
            out_copy(k, i).wait()


def update_slots(placement, plan, weight, first, second, grads):
    slots, rows, columns = weight.shape
    smem = pl.BlockSpec(memory_space=pltpu.SMEM)
    anywhere = pl.BlockSpec(memory_space=pl.ANY)
    return pl.pallas_call(
        tail_kernel,
        out_shape=[jax.ShapeDtypeStruct(weight.shape, jnp.bfloat16)] * 3,
        in_specs=[smem, smem, anywhere, anywhere, anywhere, anywhere],
        out_specs=[anywhere] * 3,
        scratch_shapes=[
            pltpu.VMEM((3, slots, rows, columns), jnp.bfloat16),
            pltpu.VMEM((slots, rows, columns), jnp.bfloat16),
            pltpu.VMEM((3, slots, rows, columns), jnp.bfloat16),
            pltpu.SemaphoreType.DMA((4,)),
            pltpu.SemaphoreType.DMA((slots,)),
            pltpu.SemaphoreType.DMA((slots,)),
            pltpu.SemaphoreType.DMA((3, slots)),
            pltpu.SemaphoreType.DMA((3, slots)),
        ],
        compiler_params=pltpu.CompilerParams(
            collective_id=0, has_side_effects=True, vmem_limit_bytes=32 * 2**20
        ),
        cost_estimate=pl.CostEstimate(
            flops=30 * weight.size, bytes_accessed=200 * weight.size, transcendentals=weight.size
        ),
    )(placement, plan, weight, first, second, grads)


def per_device(
    tokens,
    cotangent,
    routes,
    route_weight,
    gate_weight,
    up_weight,
    down_weight,
    first_moment,
    second_moment,
    placement,
    migration_plan,
):
    slot_count = lax.axis_size("expert")
    device_index = lax.axis_index("expert")
    tok_rows, quarter = tokens.shape
    per_token = routes.shape[1]
    capacity = min(tok_rows, 3 * tok_rows * per_token // (2 * slot_count))
    buffer_size = slot_count * capacity
    scale_in = 1.0 / math.sqrt(D)
    scale_mid = 1.0 / math.sqrt(FF)
    source = jnp.full((tok_rows,), device_index, jnp.int32)
    slot_ids = choose_slots(routes, placement, source)
    position = place_rows(slot_ids, slot_count)
    target = slot_ids * capacity + position
    buffer_slots = jnp.arange(buffer_size, dtype=jnp.int32)
    landing = target[None, :, :] == buffer_slots[:, None, None]
    selection = jnp.any(landing, -1).astype(jnp.bfloat16)
    row_weight = jnp.sum(jnp.where(landing, route_weight[None], jnp.float32(0.0)), (1, 2))
    sent_rows = jnp.dot(selection, tokens, preferred_element_type=jnp.float32).astype(jnp.bfloat16)
    picked_grads = jnp.dot(selection, cotangent, preferred_element_type=jnp.float32)
    sent_grads = (row_weight[:, None] * picked_grads).astype(jnp.bfloat16)
    sent_rows = sent_rows.reshape(slot_count, capacity, quarter)
    sent_grads = sent_grads.reshape(slot_count, capacity, quarter)
    got_rows, got_grads = (
        lax.all_to_all(sent_rows, "expert", split_axis=0, concat_axis=0, tiled=True),
        lax.all_to_all(sent_grads, "expert", split_axis=0, concat_axis=0, tiled=True),
    )
    def exchange(array):
        split = array.reshape(slot_count, array.shape[-2] // slot_count, array.shape[-1])
        return lax.all_to_all(split, "expert", split_axis=0, concat_axis=0, tiled=True)

    state_parts = [exchange(array[0]) for array in (gate_weight, first_moment, second_moment)]
    inputs = lax.all_gather(got_rows.reshape(buffer_size, quarter), "dp", axis=1, tiled=True)
    inputs, *state_parts[:2] = lax.optimization_barrier((inputs, *state_parts[:2]))
    gate_values = jnp.dot(inputs, gate_weight[0], preferred_element_type=jnp.float32) * scale_in
    up_values = jnp.dot(inputs, up_weight[0], preferred_element_type=jnp.float32) * scale_in
    hidden = (jax.nn.silu(gate_values) * up_values).astype(jnp.bfloat16)
    every_hidden = lax.all_gather(hidden, "dp", axis=1, tiled=True)
    w_down = down_weight[0]
    outputs = (
        jnp.dot(every_hidden, w_down, preferred_element_type=jnp.float32) * scale_mid
    ).astype(jnp.bfloat16)
    returned = lax.all_to_all(
        outputs.reshape(slot_count, capacity, quarter),
        "expert",
        split_axis=0,
        concat_axis=0,
        tiled=True,
    )
    returned_rows = returned.reshape(buffer_size, quarter)
    combined = jnp.zeros((tok_rows, quarter), jnp.float32)
    for route_index in range(per_token):
        rows_back = jnp.take(returned_rows, target[:, route_index], axis=0).astype(jnp.float32)
        combined = combined + route_weight[:, route_index : route_index + 1] * rows_back
    layer_output = combined.astype(jnp.bfloat16)
    partial_grad = lax.dot_general(
        got_grads.reshape(buffer_size, quarter),
        w_down,
        (((1,), (1,)), ((), ())),
        preferred_element_type=jnp.float32,
    )
    hidden_grad = (
        lax.psum_scatter(
            partial_grad.astype(jnp.bfloat16), "dp", scatter_dimension=1, tiled=True
        ).astype(jnp.float32)
        * scale_mid
    )
    sigmoid_gate = jax.nn.sigmoid(gate_values)
    gate_grad = (
        hidden_grad * up_values * sigmoid_gate * (1.0 + gate_values * (1.0 - sigmoid_gate))
    ).astype(jnp.bfloat16)
    weight_grad = (
        lax.dot_general(
            inputs, gate_grad, (((0,), (0,)), ((), ())), preferred_element_type=jnp.float32
        )
        * scale_in
    )
    grad_blocks = weight_grad.astype(jnp.bfloat16).reshape(state_parts[0].shape)
    updated = update_slots(placement, migration_plan, *state_parts, grad_blocks)
    result = [array.reshape(first_moment.shape) for array in updated]
    return (layer_output, result[0], result[1], result[2])


def solution(mesh):
    placed = (
        P("expert", "dp"),
        P("expert", "dp"),
        P("expert", None),
        P("expert", None),
        P("expert", None, "dp"),
        P("expert", None, "dp"),
        P("expert", None, "dp"),
        P("expert", None, "dp"),
        P("expert", None, "dp"),
        P(),
        P(),
    )
    return jax.shard_map(
        per_device,
        mesh=mesh,
        in_specs=placed,
        out_specs=(
            P("expert", "dp"),
            P("expert", None, "dp"),
            P("expert", None, "dp"),
            P("expert", None, "dp"),
        ),
        check_vma=False,
    )
```

```python
import math

import jax
import jax.numpy as jnp
from jax import lax
from jax.experimental import pallas as pl
from jax.experimental.pallas import tpu as pltpu
from jax.sharding import PartitionSpec as P

D = 3584
FF = 1024
MESH = pl.DeviceIdType.MESH


beta_first = 0.9
beta_second = 0.95
learn_rate = 0.02
weight_decay = 0.1
epsilon = 1e-08


def choose_slots(routes, placement, source):
    slot_iota = jnp.arange(placement.shape[0], dtype=jnp.int32)
    hosting = routes[..., None] == placement
    copies = jnp.sum(hosting, -1)
    earlier = (placement[:, None] == placement[None, :]) & (slot_iota[:, None] < slot_iota[None, :])
    replica_rank = jnp.sum(earlier, 0)
    replica = source[:, None] % copies
    matched = hosting & (replica_rank == replica[..., None])
    return jnp.sum(jnp.where(matched, slot_iota, 0), -1)


def place_rows(slot_ids, slot_count):
    tok_rows, per_token = slot_ids.shape
    flattened = slot_ids.reshape(-1)
    onehot = (flattened[:, None] == jnp.arange(slot_count, dtype=jnp.int32)).astype(jnp.int32)
    count = flattened.shape[0]
    order = jnp.arange(count, dtype=jnp.int32)
    upto = (order[:, None] >= order[None, :]).astype(jnp.bfloat16)
    running = jnp.dot(
        upto, onehot.astype(jnp.bfloat16), preferred_element_type=jnp.float32
    ).astype(jnp.int32)
    return (jnp.sum(running * onehot, 1) - 1).reshape(tok_rows, per_token)


def adam_update(gradient, weight, first_old, second):
    moment_one = beta_first * first_old.astype(jnp.float32) + (1.0 - beta_first) * gradient
    moment_two = (
        beta_second * second.astype(jnp.float32) + (1.0 - beta_second) * gradient * gradient
    )
    updated = weight.astype(jnp.float32) * (
        1.0 - learn_rate * weight_decay
    ) - learn_rate * moment_one / (jnp.sqrt(moment_two) + epsilon)
    return (
        updated.astype(jnp.bfloat16),
        moment_one.astype(jnp.bfloat16),
        moment_two.astype(jnp.bfloat16),
    )


def tail_kernel(
    placement_ref, plan_ref, weight_ref, first_ref, second_ref, grad_ref,
    out_w, out_1, out_2,
    state, got, staged, load_sem, grad_send, grad_recv, out_send, out_recv,
):
    slots, rows, columns = got.shape
    me = lax.axis_index("expert")
    outs = (out_w, out_1, out_2)
    chunk = math.gcd(rows, 112)

    loads = [
        pltpu.make_async_copy(ref, state.at[i], load_sem.at[i])
        for i, ref in enumerate((weight_ref, first_ref, second_ref))
    ]
    for load in loads:
        load.start()
    own = pltpu.make_async_copy(grad_ref.at[me], got.at[me], load_sem.at[3])
    own.start()

    barrier = pltpu.get_barrier_semaphore()

    @pl.loop(1, slots)
    def _(k):
        pl.semaphore_signal(
            barrier, inc=1, device_id={"expert": lax.rem(me + k, slots)}, device_id_type=MESH
        )

    pl.semaphore_wait(barrier, slots - 1)

    def grad_copy(k):
        peer = lax.rem(me + k, slots)
        return pltpu.make_async_remote_copy(
            src_ref=grad_ref.at[peer],
            dst_ref=got.at[me],
            send_sem=grad_send.at[k],
            recv_sem=grad_recv.at[k],
            device_id={"expert": peer},
            device_id_type=MESH,
        )

    def out_copy(k, i):
        return pltpu.make_async_remote_copy(
            src_ref=staged.at[i, k],
            dst_ref=outs[i].at[me],
            send_sem=out_send.at[i, k],
            recv_sem=out_recv.at[i, k],
            device_id={"expert": lax.rem(me + k, slots)},
            device_id_type=MESH,
        )

    @pl.loop(1, slots)
    def _(k):
        grad_copy(k).start()

    for load in loads:
        load.wait()
    own.wait()

    @pl.loop(1, slots)
    def _(k):
        grad_copy(k).wait()

    def work_out(k):
        old = plan_ref[lax.rem(me + k, slots)]
        held = placement_ref[old]
        shares = [
            jnp.where(placement_ref[slot] == held, 1.0, 0.0).astype(jnp.float32)
            for slot in range(slots)
        ]

        @pl.loop(0, rows // chunk)
        def _(step):
            part = pl.ds(pl.multiple_of(step * chunk, chunk), chunk)
            gradient = jnp.zeros((chunk, columns), jnp.float32)
            for slot in range(slots):
                gradient = gradient + shares[slot] * got[slot, part].astype(jnp.float32)
            staged[0, k, part], staged[1, k, part], staged[2, k, part] = adam_update(
                gradient, state[0, old, part], state[1, old, part], state[2, old, part]
            )

    @pl.loop(1, slots)
    def _(k):
        work_out(k)
        for i in range(3):
            out_copy(k, i).start()

    work_out(0)
    kept = [
        pltpu.make_async_copy(staged.at[i, 0], outs[i].at[me], load_sem.at[i]) for i in range(3)
    ]
    for copy in kept:
        copy.start()
    for copy in kept:
        copy.wait()

    @pl.loop(1, slots)
    def _(k):
        for i in range(3):
            out_copy(k, i).wait()


def update_slots(placement, plan, weight, first, second, grads):
    slots, rows, columns = weight.shape
    smem = pl.BlockSpec(memory_space=pltpu.SMEM)
    anywhere = pl.BlockSpec(memory_space=pl.ANY)
    return pl.pallas_call(
        tail_kernel,
        out_shape=[jax.ShapeDtypeStruct(weight.shape, jnp.bfloat16)] * 3,
        in_specs=[smem, smem, anywhere, anywhere, anywhere, anywhere],
        out_specs=[anywhere] * 3,
        scratch_shapes=[
            pltpu.VMEM((3, slots, rows, columns), jnp.bfloat16),
            pltpu.VMEM((slots, rows, columns), jnp.bfloat16),
            pltpu.VMEM((3, slots, rows, columns), jnp.bfloat16),
            pltpu.SemaphoreType.DMA((4,)),
            pltpu.SemaphoreType.DMA((slots,)),
            pltpu.SemaphoreType.DMA((slots,)),
            pltpu.SemaphoreType.DMA((3, slots)),
            pltpu.SemaphoreType.DMA((3, slots)),
        ],
        compiler_params=pltpu.CompilerParams(
            collective_id=0, has_side_effects=True, vmem_limit_bytes=32 * 2**20
        ),
        cost_estimate=pl.CostEstimate(
            flops=30 * weight.size, bytes_accessed=200 * weight.size, transcendentals=weight.size
        ),
    )(placement, plan, weight, first, second, grads)


def per_device(
    tokens,
    cotangent,
    routes,
    route_weight,
    gate_weight,
    up_weight,
    down_weight,
    first_moment,
    second_moment,
    placement,
    migration_plan,
):
    slot_count = lax.axis_size("expert")
    device_index = lax.axis_index("expert")
    tok_rows, quarter = tokens.shape
    per_token = routes.shape[1]
    capacity = min(tok_rows, 3 * tok_rows * per_token // (2 * slot_count))
    buffer_size = slot_count * capacity
    scale_in = 1.0 / math.sqrt(D)
    scale_mid = 1.0 / math.sqrt(FF)
    source = jnp.full((tok_rows,), device_index, jnp.int32)
    slot_ids = choose_slots(routes, placement, source)
    position = place_rows(slot_ids, slot_count)
    target = slot_ids * capacity + position
    buffer_slots = jnp.arange(buffer_size, dtype=jnp.int32)
    landing = target[None, :, :] == buffer_slots[:, None, None]
    selection = jnp.any(landing, -1).astype(jnp.bfloat16)
    row_weight = jnp.sum(jnp.where(landing, route_weight[None], jnp.float32(0.0)), (1, 2))
    cut = quarter // 256 * 128
    kept = quarter - cut
    late = jnp.dot(selection, tokens[:, :kept], preferred_element_type=jnp.float32)
    wide = lax.all_gather(tokens[:, kept:], "dp", axis=1, tiled=True)
    early = jnp.dot(selection, wide, preferred_element_type=jnp.float32).astype(jnp.bfloat16)
    picked_grads = jnp.dot(selection, cotangent, preferred_element_type=jnp.float32)
    sent_grads = (row_weight[:, None] * picked_grads).astype(jnp.bfloat16)

    def trade(rows):
        blocks = rows.reshape(slot_count, rows.shape[0] // slot_count, rows.shape[1])
        return lax.all_to_all(blocks, "expert", split_axis=0, concat_axis=0, tiled=True)

    got_late = trade(late.astype(jnp.bfloat16)).reshape(buffer_size, kept)
    got_late, sent_grads = lax.optimization_barrier((got_late, sent_grads))
    late = lax.all_gather(got_late, "dp", axis=1, tiled=True)
    got_grads = trade(sent_grads)
    got_grads, early = lax.optimization_barrier((got_grads, early))
    early = trade(early).reshape(buffer_size, wide.shape[1])
    early, *states = lax.optimization_barrier((early, gate_weight, first_moment, second_moment))
    state_parts = [trade(array[0]) for array in states]
    pieces = []
    for part in range(lax.axis_size("dp")):
        pieces.append(late[:, part * kept : (part + 1) * kept])
        pieces.append(early[:, part * cut : (part + 1) * cut])
    inputs = jnp.concatenate(pieces, axis=1)
    gate_values = jnp.dot(inputs, gate_weight[0], preferred_element_type=jnp.float32) * scale_in
    up_values = jnp.dot(inputs, up_weight[0], preferred_element_type=jnp.float32) * scale_in
    hidden = (jax.nn.silu(gate_values) * up_values).astype(jnp.bfloat16)
    every_hidden = lax.all_gather(hidden, "dp", axis=1, tiled=True)
    every_hidden, *state_parts = lax.optimization_barrier((every_hidden, *state_parts))
    w_down = down_weight[0]
    outputs = (
        jnp.dot(every_hidden, w_down, preferred_element_type=jnp.float32) * scale_mid
    ).astype(jnp.bfloat16)
    returned = lax.all_to_all(
        outputs.reshape(slot_count, capacity, quarter),
        "expert",
        split_axis=0,
        concat_axis=0,
        tiled=True,
    )
    returned_rows = returned.reshape(buffer_size, quarter)
    combined = jnp.zeros((tok_rows, quarter), jnp.float32)
    for route_index in range(per_token):
        rows_back = jnp.take(returned_rows, target[:, route_index], axis=0).astype(jnp.float32)
        combined = combined + route_weight[:, route_index : route_index + 1] * rows_back
    layer_output = combined.astype(jnp.bfloat16)
    partial_grad = lax.dot_general(
        got_grads.reshape(buffer_size, quarter),
        w_down,
        (((1,), (1,)), ((), ())),
        preferred_element_type=jnp.float32,
    )
    hidden_grad = (
        lax.psum_scatter(
            partial_grad.astype(jnp.bfloat16), "dp", scatter_dimension=1, tiled=True
        ).astype(jnp.float32)
        * scale_mid
    )
    sigmoid_gate = jax.nn.sigmoid(gate_values)
    gate_grad = (
        hidden_grad * up_values * sigmoid_gate * (1.0 + gate_values * (1.0 - sigmoid_gate))
    ).astype(jnp.bfloat16)
    weight_grad = (
        lax.dot_general(
            inputs, gate_grad, (((0,), (0,)), ((), ())), preferred_element_type=jnp.float32
        )
        * scale_in
    )
    grad_blocks = weight_grad.astype(jnp.bfloat16).reshape(state_parts[0].shape)
    updated = update_slots(placement, migration_plan, *state_parts, grad_blocks)
    result = [array.reshape(first_moment.shape) for array in updated]
    return (layer_output, result[0], result[1], result[2])


def solution(mesh):
    placed = (
        P("expert", "dp"),
        P("expert", "dp"),
        P("expert", None),
        P("expert", None),
        P("expert", None, "dp"),
        P("expert", None, "dp"),
        P("expert", None, "dp"),
        P("expert", None, "dp"),
        P("expert", None, "dp"),
        P(),
        P(),
    )
    return jax.shard_map(
        per_device,
        mesh=mesh,
        in_specs=placed,
        out_specs=(
            P("expert", "dp"),
            P("expert", None, "dp"),
            P("expert", None, "dp"),
            P("expert", None, "dp"),
        ),
        check_vma=False,
    )
```

```python
import math

import jax
import jax.numpy as jnp
from jax import lax
from jax.experimental import pallas as pl
from jax.experimental.pallas import tpu as pltpu
from jax.sharding import PartitionSpec as P

D = 3584
FF = 1024
MESH = pl.DeviceIdType.MESH


beta_first = 0.9
beta_second = 0.95
learn_rate = 0.02
weight_decay = 0.1
epsilon = 1e-08


def choose_slots(routes, placement, source):
    slot_iota = jnp.arange(placement.shape[0], dtype=jnp.int32)
    hosting = routes[..., None] == placement
    copies = jnp.sum(hosting, -1)
    earlier = (placement[:, None] == placement[None, :]) & (slot_iota[:, None] < slot_iota[None, :])
    replica_rank = jnp.sum(earlier, 0)
    replica = source[:, None] % copies
    matched = hosting & (replica_rank == replica[..., None])
    return jnp.sum(jnp.where(matched, slot_iota, 0), -1)


def place_rows(slot_ids, slot_count):
    tok_rows, per_token = slot_ids.shape
    flattened = slot_ids.reshape(-1)
    onehot = (flattened[:, None] == jnp.arange(slot_count, dtype=jnp.int32)).astype(jnp.int32)
    count = flattened.shape[0]
    order = jnp.arange(count, dtype=jnp.int32)
    upto = (order[:, None] >= order[None, :]).astype(jnp.bfloat16)
    running = jnp.dot(
        upto, onehot.astype(jnp.bfloat16), preferred_element_type=jnp.float32
    ).astype(jnp.int32)
    return (jnp.sum(running * onehot, 1) - 1).reshape(tok_rows, per_token)


def adam_update(gradient, weight, first_old, second):
    moment_one = beta_first * first_old.astype(jnp.float32) + (1.0 - beta_first) * gradient
    moment_two = (
        beta_second * second.astype(jnp.float32) + (1.0 - beta_second) * gradient * gradient
    )
    updated = weight.astype(jnp.float32) * (
        1.0 - learn_rate * weight_decay
    ) - learn_rate * moment_one / (jnp.sqrt(moment_two) + epsilon)
    return (
        updated.astype(jnp.bfloat16),
        moment_one.astype(jnp.bfloat16),
        moment_two.astype(jnp.bfloat16),
    )


def tail_kernel(
    placement_ref, plan_ref, weight_ref, first_ref, second_ref, grad_ref,
    out_w, out_1, out_2,
    state, got, staged, load_sem, grad_send, grad_recv, out_send, out_recv,
):
    slots, rows, columns = got.shape
    me = lax.axis_index("expert")
    outs = (out_w, out_1, out_2)
    chunk = math.gcd(rows, 112)

    loads = [
        pltpu.make_async_copy(ref, state.at[i], load_sem.at[i])
        for i, ref in enumerate((weight_ref, first_ref, second_ref))
    ]
    for load in loads:
        load.start()
    own = pltpu.make_async_copy(grad_ref.at[me], got.at[me], load_sem.at[3])
    own.start()

    barrier = pltpu.get_barrier_semaphore()

    @pl.loop(1, slots)
    def _(k):
        pl.semaphore_signal(
            barrier, inc=1, device_id={"expert": lax.rem(me + k, slots)}, device_id_type=MESH
        )

    pl.semaphore_wait(barrier, slots - 1)

    def grad_copy(k):
        peer = lax.rem(me + k, slots)
        return pltpu.make_async_remote_copy(
            src_ref=grad_ref.at[peer],
            dst_ref=got.at[me],
            send_sem=grad_send.at[k],
            recv_sem=grad_recv.at[k],
            device_id={"expert": peer},
            device_id_type=MESH,
        )

    def out_copy(k, i):
        return pltpu.make_async_remote_copy(
            src_ref=staged.at[i, k],
            dst_ref=outs[i].at[me],
            send_sem=out_send.at[i, k],
            recv_sem=out_recv.at[i, k],
            device_id={"expert": lax.rem(me + k, slots)},
            device_id_type=MESH,
        )

    @pl.loop(1, slots)
    def _(k):
        grad_copy(k).start()

    for load in loads:
        load.wait()
    own.wait()

    @pl.loop(1, slots)
    def _(k):
        grad_copy(k).wait()

    def work_out(k):
        old = plan_ref[lax.rem(me + k, slots)]
        held = placement_ref[old]
        shares = [
            jnp.where(placement_ref[slot] == held, 1.0, 0.0).astype(jnp.float32)
            for slot in range(slots)
        ]

        @pl.loop(0, rows // chunk)
        def _(step):
            part = pl.ds(pl.multiple_of(step * chunk, chunk), chunk)
            gradient = jnp.zeros((chunk, columns), jnp.float32)
            for slot in range(slots):
                gradient = gradient + shares[slot] * got[slot, part].astype(jnp.float32)
            staged[0, k, part], staged[1, k, part], staged[2, k, part] = adam_update(
                gradient, state[0, old, part], state[1, old, part], state[2, old, part]
            )

    @pl.loop(1, slots)
    def _(k):
        work_out(k)
        for i in range(3):
            out_copy(k, i).start()

    work_out(0)
    kept = [
        pltpu.make_async_copy(staged.at[i, 0], outs[i].at[me], load_sem.at[i]) for i in range(3)
    ]
    for copy in kept:
        copy.start()
    for copy in kept:
        copy.wait()

    @pl.loop(1, slots)
    def _(k):
        for i in range(3):
            out_copy(k, i).wait()


def update_slots(placement, plan, weight, first, second, grads):
    slots, rows, columns = weight.shape
    smem = pl.BlockSpec(memory_space=pltpu.SMEM)
    anywhere = pl.BlockSpec(memory_space=pl.ANY)
    return pl.pallas_call(
        tail_kernel,
        out_shape=[jax.ShapeDtypeStruct(weight.shape, jnp.bfloat16)] * 3,
        in_specs=[smem, smem, anywhere, anywhere, anywhere, anywhere],
        out_specs=[anywhere] * 3,
        scratch_shapes=[
            pltpu.VMEM((3, slots, rows, columns), jnp.bfloat16),
            pltpu.VMEM((slots, rows, columns), jnp.bfloat16),
            pltpu.VMEM((3, slots, rows, columns), jnp.bfloat16),
            pltpu.SemaphoreType.DMA((4,)),
            pltpu.SemaphoreType.DMA((slots,)),
            pltpu.SemaphoreType.DMA((slots,)),
            pltpu.SemaphoreType.DMA((3, slots)),
            pltpu.SemaphoreType.DMA((3, slots)),
        ],
        compiler_params=pltpu.CompilerParams(
            collective_id=0, has_side_effects=True, vmem_limit_bytes=32 * 2**20
        ),
        cost_estimate=pl.CostEstimate(
            flops=30 * weight.size, bytes_accessed=200 * weight.size, transcendentals=weight.size
        ),
    )(placement, plan, weight, first, second, grads)


def per_device(
    tokens,
    cotangent,
    routes,
    route_weight,
    gate_weight,
    up_weight,
    down_weight,
    first_moment,
    second_moment,
    placement,
    migration_plan,
):
    slot_count = lax.axis_size("expert")
    device_index = lax.axis_index("expert")
    tok_rows, quarter = tokens.shape
    per_token = routes.shape[1]
    capacity = min(tok_rows, 3 * tok_rows * per_token // (2 * slot_count))
    buffer_size = slot_count * capacity
    scale_in = 1.0 / math.sqrt(D)
    scale_mid = 1.0 / math.sqrt(FF)
    source = jnp.full((tok_rows,), device_index, jnp.int32)
    slot_ids = choose_slots(routes, placement, source)
    position = place_rows(slot_ids, slot_count)
    target = slot_ids * capacity + position
    buffer_slots = jnp.arange(buffer_size, dtype=jnp.int32)
    landing = target[None, :, :] == buffer_slots[:, None, None]
    selection = jnp.any(landing, -1).astype(jnp.bfloat16)
    row_weight = jnp.sum(jnp.where(landing, route_weight[None], jnp.float32(0.0)), (1, 2))
    cut = quarter // 384 * 128
    kept = quarter - cut
    late = jnp.dot(selection, tokens[:, :kept], preferred_element_type=jnp.float32)
    wide = lax.all_gather(tokens[:, kept:], "dp", axis=1, tiled=True)
    early = jnp.dot(selection, wide, preferred_element_type=jnp.float32).astype(jnp.bfloat16)
    picked_grads = jnp.dot(selection, cotangent, preferred_element_type=jnp.float32)
    sent_grads = (row_weight[:, None] * picked_grads).astype(jnp.bfloat16)

    def trade(rows):
        blocks = rows.reshape(slot_count, rows.shape[0] // slot_count, rows.shape[1])
        return lax.all_to_all(blocks, "expert", split_axis=0, concat_axis=0, tiled=True)

    got_late = trade(late.astype(jnp.bfloat16)).reshape(buffer_size, kept)
    got_late, sent_grads = lax.optimization_barrier((got_late, sent_grads))
    late = lax.all_gather(got_late, "dp", axis=1, tiled=True)
    got_grads = trade(sent_grads)
    got_grads, early = lax.optimization_barrier((got_grads, early))
    early = trade(early).reshape(buffer_size, wide.shape[1])
    early, *states = lax.optimization_barrier((early, gate_weight, first_moment, second_moment))
    state_parts = [trade(array[0]) for array in states]
    pieces = []
    for part in range(lax.axis_size("dp")):
        pieces.append(late[:, part * kept : (part + 1) * kept])
        pieces.append(early[:, part * cut : (part + 1) * cut])
    inputs = jnp.concatenate(pieces, axis=1)
    gate_values = jnp.dot(inputs, gate_weight[0], preferred_element_type=jnp.float32) * scale_in
    up_values = jnp.dot(inputs, up_weight[0], preferred_element_type=jnp.float32) * scale_in
    hidden = (jax.nn.silu(gate_values) * up_values).astype(jnp.bfloat16)
    every_hidden = lax.all_gather(hidden, "dp", axis=1, tiled=True)
    every_hidden, *state_parts = lax.optimization_barrier((every_hidden, *state_parts))
    w_down = down_weight[0]
    outputs = (
        jnp.dot(every_hidden, w_down, preferred_element_type=jnp.float32) * scale_mid
    ).astype(jnp.bfloat16)
    returned = lax.all_to_all(
        outputs.reshape(slot_count, capacity, quarter),
        "expert",
        split_axis=0,
        concat_axis=0,
        tiled=True,
    )
    returned_rows = returned.reshape(buffer_size, quarter)
    combined = jnp.zeros((tok_rows, quarter), jnp.float32)
    for route_index in range(per_token):
        rows_back = jnp.take(returned_rows, target[:, route_index], axis=0).astype(jnp.float32)
        combined = combined + route_weight[:, route_index : route_index + 1] * rows_back
    layer_output = combined.astype(jnp.bfloat16)
    partial_grad = lax.dot_general(
        got_grads.reshape(buffer_size, quarter),
        w_down,
        (((1,), (1,)), ((), ())),
        preferred_element_type=jnp.float32,
    )
    hidden_grad = (
        lax.psum_scatter(
            partial_grad.astype(jnp.bfloat16), "dp", scatter_dimension=1, tiled=True
        ).astype(jnp.float32)
        * scale_mid
    )
    sigmoid_gate = jax.nn.sigmoid(gate_values)
    gate_grad = (
        hidden_grad * up_values * sigmoid_gate * (1.0 + gate_values * (1.0 - sigmoid_gate))
    ).astype(jnp.bfloat16)
    weight_grad = (
        lax.dot_general(
            inputs, gate_grad, (((0,), (0,)), ((), ())), preferred_element_type=jnp.float32
        )
        * scale_in
    )
    grad_blocks = weight_grad.astype(jnp.bfloat16).reshape(state_parts[0].shape)
    updated = update_slots(placement, migration_plan, *state_parts, grad_blocks)
    result = [array.reshape(first_moment.shape) for array in updated]
    return (layer_output, result[0], result[1], result[2])


def solution(mesh):
    placed = (
        P("expert", "dp"),
        P("expert", "dp"),
        P("expert", None),
        P("expert", None),
        P("expert", None, "dp"),
        P("expert", None, "dp"),
        P("expert", None, "dp"),
        P("expert", None, "dp"),
        P("expert", None, "dp"),
        P(),
        P(),
    )
    return jax.shard_map(
        per_device,
        mesh=mesh,
        in_specs=placed,
        out_specs=(
            P("expert", "dp"),
            P("expert", None, "dp"),
            P("expert", None, "dp"),
            P("expert", None, "dp"),
        ),
        check_vma=False,
    )
```
